32 devices in a mesh: dp: 4 (over y, x), row: 2 (over core), col: 4 (over z).
Axes of the slice: x: 2, y: 2, z: 4, core: 2. Of those that a mesh axis runs over, the one named last changes fastest.
Arguments:
- attn_heads: bfloat16 [12288, 2304], P(('dp', 'col'), 'row'), may hold values from -6 to 6
- out_weight: bfloat16 [2304, 4096], P('row', 'col'), may hold values from -0.125 to 0.125
- cotangent: bfloat16 [12288, 4096], P(('dp', 'row'), 'col'), may hold values from -6 to 6
Outputs:
- head_grad: bfloat16 [12288, 2304], P(('dp', 'col'), 'row')
- weight_grad: float32 [2304, 4096], P('row', 'col')
The draws below stay inside these ranges and needn't reach their ends.
All inputs are finite; a program needn't handle non-finite values.
Results may differ from the reference program's by a relative error of at most 0.015.
Values may be sent and summed in bfloat16 or wider, within the bound.
A program may use at most 64 MiB of HBM per device.

```python
import jax
import jax.numpy as jnp
from jax import lax

D = 4096
HQ = 2304
TOKENS = 12288
N_COL = 4


def levels(own_key, dims, split, least, high):
    factor_of = 1.0
    for position, parts in split:
        heights = jax.random.uniform(jax.random.fold_in(jax.random.fold_in(own_key, 6), position), (parts,), jnp.float32, least / len(split), high / len(split))
        factor_of = factor_of * jnp.repeat(jnp.exp(heights), dims[position] // parts).reshape((-1,) + (1,) * (len(dims) - 1 - position))
    return factor_of


def noise(key, extent, spread, bound, split=(), kind=jnp.bfloat16):
    drawn = jax.random.normal(key, extent, jnp.float32) * spread
    if len(split) > 0:
        drawn = levels(key, extent, split, -0.22, 0.18) * drawn
    return jnp.clip(drawn, min=-bound, max=bound).astype(kind)


def setup_inputs(seed: int = 0) -> dict:
    splits = jax.random.split(jax.random.key(seed), 4)
    return {
        "attn_heads": noise(splits[0], (TOKENS, HQ), 1.0, 6.0, ((0, 16), (1, 2))),
        "out_weight": noise(splits[1], (HQ, D), HQ ** -0.5, 0.125, ((0, 2), (1, 4))),
        "cotangent": noise(splits[2], (TOKENS, D), 1.0, 6.0, ((0, 8), (1, 4))),
    }


def reference(attn_heads, out_weight, cotangent):
    width = D // N_COL
    head_sum = jnp.zeros((TOKENS, HQ), jnp.float32)
    for block in range(N_COL):
        cot_block = cotangent[:, block * width:(block + 1) * width]
        weight_block = out_weight[:, block * width:(block + 1) * width]
        partial_block = lax.dot_general(cot_block, weight_block, (((1,), (1,)), ((), ())), preferred_element_type=jnp.float32)
        head_sum = head_sum + partial_block.astype(jnp.bfloat16).astype(jnp.float32)
    head_grad = head_sum.astype(jnp.bfloat16)
    grad_scale = float(TOKENS) ** -0.5
    weight_grad = lax.dot_general(attn_heads, cotangent, (((0,), (0,)), ((), ())), preferred_element_type=jnp.float32) * grad_scale
    return head_grad, weight_grad
```

```python
import functools

import jax
import jax.numpy as jnp
from jax import lax
from jax.experimental import pallas as pl
from jax.experimental.pallas import tpu as pltpu
from jax.sharding import PartitionSpec as P

MESH = pl.DeviceIdType.MESH
TILE = 256


def kernel(n, n_row, n_dp, sum_dp, chunks, heads_ref, weight_ref, cot_ref, head_ref, wg_ref,
           heads_all, cot_all, weight, part, run, acc, wg_send, dp_recv, local_sem,
           z_send, z_recv, row_send, row_recv, rs_send, rs_recv, ag_send, ag_recv):
    c, r, d = lax.axis_index("col"), lax.axis_index("row"), lax.axis_index("dp")
    tok, hq = heads_ref.shape
    wide = hq // chunks
    cot_rows, feat = cot_ref.shape
    piece = wide // n_dp

    barrier = pltpu.get_barrier_semaphore()

    @pl.when(c > 0)
    def _():
        pl.semaphore_signal(barrier, inc=1, device_id={"col": c - 1}, device_id_type=MESH)

    @pl.when(c < n - 1)
    def _():
        pl.semaphore_signal(barrier, inc=1, device_id={"col": c + 1}, device_id_type=MESH)

    for o in range(1, n_row):
        pl.semaphore_signal(barrier, inc=1, device_id={"row": lax.rem(r + o, n_row)}, device_id_type=MESH)
    if sum_dp:
        for o in range(1, n_dp):
            pl.semaphore_signal(barrier, inc=1, device_id={"dp": lax.rem(d + o, n_dp)}, device_id_type=MESH)
    others = (n_row - 1) + (n_dp - 1 if sum_dp else 0)
    pl.semaphore_wait(barrier, others + (c > 0).astype(jnp.int32) + (c < n - 1).astype(jnp.int32))

    def z_copy(way, j, k, src, dst):
        to = jnp.clip(c + 1 - 2 * way, 0, n - 1)
        return pltpu.make_async_remote_copy(
            src_ref=src, dst_ref=dst, send_sem=z_send.at[way, j, k], recv_sem=z_recv.at[way, j, k],
            device_id={"col": to}, device_id_type=MESH)

    def row_copy(o):
        at = pl.ds(pl.multiple_of(r * cot_rows, cot_rows), cot_rows)
        return pltpu.make_async_remote_copy(
            src_ref=cot_ref, dst_ref=cot_all.at[at], send_sem=row_send.at[o], recv_sem=row_recv.at[o],
            device_id={"row": lax.rem(r + o, n_row)}, device_id_type=MESH)

    for o in range(1, n_row):
        row_copy(o).start()
    own_cot = pltpu.make_async_copy(
        cot_ref, cot_all.at[pl.ds(pl.multiple_of(r * cot_rows, cot_rows), cot_rows)], local_sem.at[0])
    own_cot.start()
    own_weight = pltpu.make_async_copy(weight_ref, weight, local_sem.at[1])
    own_weight.start()

    def heads_chunk(k):
        return heads_ref.at[:, pl.ds(k * wide, wide)]

    for k in range(chunks):
        @pl.when(c < n - 1)
        def _():
            z_copy(0, 0, k, heads_chunk(k), heads_all.at[c, k]).start()

        @pl.when(c > 0)
        def _():
            z_copy(1, 0, k, heads_chunk(k), heads_all.at[c, k]).start()

    own_heads = [pltpu.make_async_copy(heads_chunk(k), heads_all.at[c, k], local_sem.at[2 + k])
                 for k in range(chunks)]
    for copy in own_heads:
        copy.start()
    own_weight.wait()
    own_cot.wait()
    for o in range(1, n_row):
        row_copy(o).wait_recv()

    def partials(i, carry):
        t, m = i // (tok // TILE), lax.rem(i, tok // TILE)
        rows = pl.ds(pl.multiple_of(i * TILE, TILE), TILE)
        for k in range(chunks):
            part[t, k, pl.ds(pl.multiple_of(m * TILE, TILE), TILE), :] = lax.dot_general(
                cot_all[rows, :], weight[k * wide:(k + 1) * wide, :], (((1,), (1,)), ((), ())),
                preferred_element_type=jnp.float32).astype(jnp.bfloat16)
        return carry

    lax.fori_loop(0, n * tok // TILE, partials, 0)
    for copy in own_heads:
        copy.wait()

    def add_rows(way, j, k, t):
        def body(m, carry):
            rows = pl.ds(pl.multiple_of(m * TILE, TILE), TILE)
            run[way, j, k, rows, :] = (run[way, j, k, rows, :].astype(jnp.float32)
                                       + part[t, k, rows, :].astype(jnp.float32)).astype(jnp.bfloat16)
            return carry
        lax.fori_loop(0, tok // TILE, body, 0)

    def arrive(way, j, k):
        p = c if way == 0 else n - 1 - c

        def shard(q):
            return q if way == 0 else n - 1 - q

        @pl.when(jnp.logical_and(p > 0, j < p))
        def _():
            s = jnp.clip(shard(p - 1 - j), 0, n - 1)
            z_copy(way, j, k, heads_all.at[s, k], heads_all.at[s, k]).wait_recv()
            if j < n - 1:
                @pl.when(p < n - 1)
                def _():
                    z_copy(way, j + 1, k, heads_all.at[s, k], heads_all.at[s, k]).start()

        @pl.when(jnp.logical_and(p > 0, j >= p))
        def _():
            z_copy(way, j, k, run.at[way, j, k], run.at[way, j, k]).wait_recv()
            if j < n - 1:
                t = jnp.clip(shard(n + p - 1 - j), 0, n - 1)
                add_rows(way, j, k, t)
                z_copy(way, j + 1, k, run.at[way, j, k], run.at[way, j + 1, k]).start()

        if j < n - 1:
            @pl.when(p == 0)
            def _():
                t = shard(n - 1 - j)
                z_copy(way, j + 1, k, part.at[t, k], run.at[way, j + 1, k]).start()

    def weight_chunk(k):
        for s in range(n):
            term = lax.dot_general(
                heads_all[s, k], cot_all[s * tok:(s + 1) * tok, :], (((0,), (0,)), ((), ())),
                preferred_element_type=jnp.float32)
            if s == 0:
                acc[...] = term
            else:
                acc[...] += term
        if not sum_dp:
            wg_ref[pl.ds(pl.multiple_of(k * wide, wide), wide), :] = acc[...].astype(jnp.bfloat16)
            return
        for q in range(n_dp):
            wg_send[k, q] = acc[q * piece:(q + 1) * piece, :].astype(jnp.bfloat16)
        for o in range(1, n_dp):
            to_owner(o, k).start()

    def to_owner(o, k):
        to = lax.rem(d + o, n_dp)
        return pltpu.make_async_remote_copy(
            src_ref=wg_send.at[k, to], dst_ref=dp_recv.at[k, o], send_sem=rs_send.at[o, k],
            recv_sem=rs_recv.at[o, k], device_id={"dp": to}, device_id_type=MESH)

    def piece_at(k, q):
        return pl.ds(pl.multiple_of(k * wide + q * piece, piece), piece)

    def from_owner(o, k):
        return pltpu.make_async_remote_copy(
            src_ref=wg_ref.at[piece_at(k, d)], dst_ref=wg_ref.at[piece_at(k, d)], send_sem=ag_send.at[o, k],
            recv_sem=ag_recv.at[o, k], device_id={"dp": lax.rem(d + o, n_dp)}, device_id_type=MESH)

    def own_piece(k):
        for o in range(1, n_dp):
            to_owner(o, k).wait_recv()
        total = wg_send[k, d].astype(jnp.float32)
        for o in range(1, n_dp):
            total = total + dp_recv[k, o].astype(jnp.float32)
        wg_ref[piece_at(k, d), :] = total.astype(jnp.bfloat16)
        for o in range(1, n_dp):
            from_owner(o, k).start()

    def finish(k):
        def body(m, carry):
            rows = pl.ds(pl.multiple_of(m * TILE, TILE), TILE)
            up = jnp.where(c > 0, run[0, n - 1, k, rows, :].astype(jnp.float32), 0.0)
            down = jnp.where(c < n - 1, run[1, n - 1, k, rows, :].astype(jnp.float32), 0.0)
            total = part[c, k, rows, :].astype(jnp.float32) + up + down
            head_ref[k, rows, :] = total.astype(jnp.bfloat16)
            return carry
        lax.fori_loop(0, tok // TILE, body, 0)

    def clear(way):
        for k in range(chunks):
            run[way, n - 1, k] = jnp.zeros_like(run[way, n - 1, k])

    pl.when(c == 0)(lambda: clear(0))
    pl.when(c == n - 1)(lambda: clear(1))

    for j in range(n):
        def step(k, carry, j=j):
            if j == n - 1 and sum_dp:
                own_piece(k)
            arrive(0, j, k)
            arrive(1, j, k)
            if j == n - 2:
                weight_chunk(k)
            if j == n - 1:
                finish(k)
            return carry
        lax.fori_loop(0, chunks, step, 0)

    def drain(k, carry):
        for j in range(n):
            @pl.when(c < n - 1)
            def _():
                z_copy(0, j, k, run.at[0, j, k], run.at[0, j, k]).wait_send()

            @pl.when(c > 0)
            def _():
                z_copy(1, j, k, run.at[1, j, k], run.at[1, j, k]).wait_send()
        if sum_dp:
            for o in range(1, n_dp):
                to_owner(o, k).wait_send()
                from_owner(o, k).wait_send()
                from_owner(o, k).wait_recv()
        return carry

    lax.fori_loop(0, chunks, drain, 0)
    for o in range(1, n_row):
        row_copy(o).wait_send()


def per_device(sizes, attn_heads, out_weight, cotangent):
    n, n_row, n_dp = sizes["col"], sizes["row"], sizes["dp"]
    tok, hq = attn_heads.shape
    feat = out_weight.shape[1]
    chunks = 3
    wide = hq // chunks
    sum_dp = wide % (16 * n_dp) == 0
    grad_scale = float(tok * n * n_dp) ** (-0.5)
    bf16, dma = jnp.bfloat16, pltpu.SemaphoreType.DMA
    piece = wide // n_dp if sum_dp else 16
    slots = n_dp if sum_dp else 1
    head_grad, weight_sum = pl.pallas_call(
        functools.partial(kernel, n, n_row, n_dp, sum_dp, chunks),
        out_shape=(jax.ShapeDtypeStruct((chunks, tok, wide), bf16), jax.ShapeDtypeStruct((hq, feat), bf16)),
        in_specs=[pl.BlockSpec(memory_space=pl.ANY)] * 3,
        out_specs=[pl.BlockSpec(memory_space=pltpu.VMEM)] * 2,
        scratch_shapes=[
            pltpu.VMEM((n, chunks, tok, wide), bf16),
            pltpu.VMEM((n * tok, feat), bf16),
            pltpu.VMEM((hq, feat), bf16),
            pltpu.VMEM((n, chunks, tok, wide), bf16),
            pltpu.VMEM((2, n, chunks, tok, wide), bf16),
            pltpu.VMEM((wide, feat), jnp.float32),
            pltpu.VMEM((chunks, slots, piece, feat), bf16),
            pltpu.VMEM((chunks, slots, piece, feat), bf16),
            dma((2 + chunks,)),
            dma((2, n, chunks)), dma((2, n, chunks)),
            dma((n_row,)), dma((n_row,)),
            dma((slots, chunks)), dma((slots, chunks)), dma((slots, chunks)), dma((slots, chunks)),
        ],
        compiler_params=pltpu.CompilerParams(
            collective_id=0, has_side_effects=True, vmem_limit_bytes=60 * 1024 * 1024),
        cost_estimate=pl.CostEstimate(
            flops=4 * n * tok * hq * feat, bytes_accessed=4 * n * tok * (hq + feat), transcendentals=0),
    )(attn_heads, out_weight, cotangent)
    head_grad = jnp.concatenate([head_grad[k] for k in range(chunks)], axis=1)
    if not sum_dp:
        weight_sum = lax.psum(weight_sum, "dp")
    return head_grad, weight_sum.astype(jnp.float32) * grad_scale


def solution(mesh):
    return jax.shard_map(
        functools.partial(per_device, dict(mesh.shape)),
        mesh=mesh,
        in_specs=(P(("dp", "col"), "row"), P("row", "col"), P(("dp", "row"), "col")),
        out_specs=(P(("dp", "col"), "row"), P("row", "col")),
        check_vma=False,
    )
```

```python
import functools

import jax
import jax.numpy as jnp
from jax import lax
from jax.experimental import pallas as pl
from jax.experimental.pallas import tpu as pltpu
from jax.sharding import PartitionSpec as P

MESH = pl.DeviceIdType.MESH
TILE = 256


def kernel(n, n_row, n_dp, sum_dp, chunks, grad_scale, heads_ref, weight_ref, cot_ref, head_ref, wg_ref,
           heads_all, cot_all, weight, part, run, acc, wg_send, dp_recv, wg_sum, local_sem,
           z_send, z_recv, row_send, row_recv, rs_send, rs_recv, ag_send, ag_recv):
    c, r, d = lax.axis_index("col"), lax.axis_index("row"), lax.axis_index("dp")
    tok, hq = heads_ref.shape
    wide = hq // chunks
    cot_rows, feat = cot_ref.shape
    piece = wide // n_dp

    barrier = pltpu.get_barrier_semaphore()

    @pl.when(c > 0)
    def _():
        pl.semaphore_signal(barrier, inc=1, device_id={"col": c - 1}, device_id_type=MESH)

    @pl.when(c < n - 1)
    def _():
        pl.semaphore_signal(barrier, inc=1, device_id={"col": c + 1}, device_id_type=MESH)

    for o in range(1, n_row):
        pl.semaphore_signal(barrier, inc=1, device_id={"row": lax.rem(r + o, n_row)}, device_id_type=MESH)
    if sum_dp:
        for o in range(1, n_dp):
            pl.semaphore_signal(barrier, inc=1, device_id={"dp": lax.rem(d + o, n_dp)}, device_id_type=MESH)
    others = (n_row - 1) + (n_dp - 1 if sum_dp else 0)
    pl.semaphore_wait(barrier, others + (c > 0).astype(jnp.int32) + (c < n - 1).astype(jnp.int32))

    def z_copy(way, j, k, src, dst):
        to = jnp.clip(c + 1 - 2 * way, 0, n - 1)
        return pltpu.make_async_remote_copy(
            src_ref=src, dst_ref=dst, send_sem=z_send.at[way, j, k], recv_sem=z_recv.at[way, j, k],
            device_id={"col": to}, device_id_type=MESH)

    def row_copy(o):
        at = pl.ds(pl.multiple_of(r * cot_rows, cot_rows), cot_rows)
        return pltpu.make_async_remote_copy(
            src_ref=cot_ref, dst_ref=cot_all.at[at], send_sem=row_send.at[o], recv_sem=row_recv.at[o],
            device_id={"row": lax.rem(r + o, n_row)}, device_id_type=MESH)

    for o in range(1, n_row):
        row_copy(o).start()
    own_cot = pltpu.make_async_copy(
        cot_ref, cot_all.at[pl.ds(pl.multiple_of(r * cot_rows, cot_rows), cot_rows)], local_sem.at[0])
    own_cot.start()
    own_weight = pltpu.make_async_copy(weight_ref, weight, local_sem.at[1])
    own_weight.start()

    def heads_chunk(k):
        return heads_ref.at[:, pl.ds(k * wide, wide)]

    for k in range(chunks):
        @pl.when(c < n - 1)
        def _():
            z_copy(0, 0, k, heads_chunk(k), heads_all.at[c, k]).start()

        @pl.when(c > 0)
        def _():
            z_copy(1, 0, k, heads_chunk(k), heads_all.at[c, k]).start()

    own_heads = [pltpu.make_async_copy(heads_chunk(k), heads_all.at[c, k], local_sem.at[2 + k])
                 for k in range(chunks)]
    for copy in own_heads:
        copy.start()
    own_weight.wait()
    own_cot.wait()
    for o in range(1, n_row):
        row_copy(o).wait_recv()

    def partials(i, carry):
        t, m = i // (tok // TILE), lax.rem(i, tok // TILE)
        rows = pl.ds(pl.multiple_of(i * TILE, TILE), TILE)
        for k in range(chunks):
            part[t, k, pl.ds(pl.multiple_of(m * TILE, TILE), TILE), :] = lax.dot_general(
                cot_all[rows, :], weight[k * wide:(k + 1) * wide, :], (((1,), (1,)), ((), ())),
                preferred_element_type=jnp.float32).astype(jnp.bfloat16)
        return carry

    lax.fori_loop(0, n * tok // TILE, partials, 0)
    for copy in own_heads:
        copy.wait()

    def add_rows(way, j, k, t):
        def body(m, carry):
            rows = pl.ds(pl.multiple_of(m * TILE, TILE), TILE)
            run[way, j, k, rows, :] = (run[way, j, k, rows, :].astype(jnp.float32)
                                       + part[t, k, rows, :].astype(jnp.float32)).astype(jnp.bfloat16)
            return carry
        lax.fori_loop(0, tok // TILE, body, 0)

    def arrive(way, j, k):
        p = c if way == 0 else n - 1 - c

        def shard(q):
            return q if way == 0 else n - 1 - q

        @pl.when(jnp.logical_and(p > 0, j < p))
        def _():
            s = jnp.clip(shard(p - 1 - j), 0, n - 1)
            z_copy(way, j, k, heads_all.at[s, k], heads_all.at[s, k]).wait_recv()
            if j < n - 1:
                @pl.when(p < n - 1)
                def _():
                    z_copy(way, j + 1, k, heads_all.at[s, k], heads_all.at[s, k]).start()

        @pl.when(jnp.logical_and(p > 0, j >= p))
        def _():
            z_copy(way, j, k, run.at[way, j, k], run.at[way, j, k]).wait_recv()
            if j < n - 1:
                t = jnp.clip(shard(n + p - 1 - j), 0, n - 1)
                add_rows(way, j, k, t)
                z_copy(way, j + 1, k, run.at[way, j, k], run.at[way, j + 1, k]).start()

        if j < n - 1:
            @pl.when(p == 0)
            def _():
                t = shard(n - 1 - j)
                z_copy(way, j + 1, k, part.at[t, k], run.at[way, j + 1, k]).start()

    def weight_chunk(k):
        for s in range(n):
            term = lax.dot_general(
                heads_all[s, k], cot_all[s * tok:(s + 1) * tok, :], (((0,), (0,)), ((), ())),
                preferred_element_type=jnp.float32)
            if s == 0:
                acc[...] = term
            else:
                acc[...] += term
        if not sum_dp:
            wg_ref[pl.ds(pl.multiple_of(k * wide, wide), wide), :] = acc[...].astype(jnp.bfloat16)
            return
        for q in range(n_dp):
            wg_send[k, q] = acc[q * piece:(q + 1) * piece, :].astype(jnp.bfloat16)
        for o in range(1, n_dp):
            to_owner(o, k).start()

    def to_owner(o, k):
        to = lax.rem(d + o, n_dp)
        return pltpu.make_async_remote_copy(
            src_ref=wg_send.at[k, to], dst_ref=dp_recv.at[k, o], send_sem=rs_send.at[o, k],
            recv_sem=rs_recv.at[o, k], device_id={"dp": to}, device_id_type=MESH)

    def from_owner(o, k):
        return pltpu.make_async_remote_copy(
            src_ref=wg_sum.at[k, d], dst_ref=wg_sum.at[k, d], send_sem=ag_send.at[o, k],
            recv_sem=ag_recv.at[o, k], device_id={"dp": lax.rem(d + o, n_dp)}, device_id_type=MESH)

    def own_piece(k):
        for o in range(1, n_dp):
            to_owner(o, k).wait_recv()
        total = wg_send[k, d].astype(jnp.float32)
        for o in range(1, n_dp):
            total = total + dp_recv[k, o].astype(jnp.float32)
        wg_sum[k, d] = total.astype(jnp.bfloat16)
        for o in range(1, n_dp):
            from_owner(o, k).start()

    def widen(k):
        for o in range(1, n_dp):
            from_owner(o, k).wait_recv()
        for q in range(n_dp):
            at = k * wide + q * piece
            wg_ref[at:at + piece, :] = wg_sum[k, q].astype(jnp.float32) * grad_scale

    def finish(k):
        def body(m, carry):
            rows = pl.ds(pl.multiple_of(m * TILE, TILE), TILE)
            up = jnp.where(c > 0, run[0, n - 1, k, rows, :].astype(jnp.float32), 0.0)
            down = jnp.where(c < n - 1, run[1, n - 1, k, rows, :].astype(jnp.float32), 0.0)
            total = part[c, k, rows, :].astype(jnp.float32) + up + down
            head_ref[rows, pl.ds(k * wide, wide)] = total.astype(jnp.bfloat16)
            return carry
        lax.fori_loop(0, tok // TILE, body, 0)

    def clear(way):
        for k in range(chunks):
            run[way, n - 1, k] = jnp.zeros_like(run[way, n - 1, k])

    pl.when(c == 0)(lambda: clear(0))
    pl.when(c == n - 1)(lambda: clear(1))

    for j in range(n - 1):
        def step(k, carry, j=j):
            arrive(0, j, k)
            arrive(1, j, k)
            if j == n - 2:
                weight_chunk(k)
            return carry
        lax.fori_loop(0, chunks, step, 0)

    for k in range(chunks):
        if sum_dp:
            for late in range(chunks):
                if max(late - 1, 0) == k:
                    own_piece(late)
            if k == chunks - 1:
                for late in range(chunks):
                    widen(late)
        arrive(0, n - 1, k)
        arrive(1, n - 1, k)
        finish(k)

    def drain(k, carry):
        for j in range(n):
            @pl.when(c < n - 1)
            def _():
                z_copy(0, j, k, run.at[0, j, k], run.at[0, j, k]).wait_send()

            @pl.when(c > 0)
            def _():
                z_copy(1, j, k, run.at[1, j, k], run.at[1, j, k]).wait_send()
        if sum_dp:
            for o in range(1, n_dp):
                to_owner(o, k).wait_send()
                from_owner(o, k).wait_send()
        return carry

    lax.fori_loop(0, chunks, drain, 0)
    for o in range(1, n_row):
        row_copy(o).wait_send()


def per_device(sizes, attn_heads, out_weight, cotangent):
    n, n_row, n_dp = sizes["col"], sizes["row"], sizes["dp"]
    tok, hq = attn_heads.shape
    feat = out_weight.shape[1]
    chunks = 3
    wide = hq // chunks
    sum_dp = wide % (16 * n_dp) == 0
    grad_scale = float(tok * n * n_dp) ** (-0.5)
    bf16, dma = jnp.bfloat16, pltpu.SemaphoreType.DMA
    piece = wide // n_dp if sum_dp else 16
    slots = n_dp if sum_dp else 1
    head_grad, weight_sum = pl.pallas_call(
        functools.partial(kernel, n, n_row, n_dp, sum_dp, chunks, grad_scale),
        out_shape=(pltpu.VMEM((tok, hq), bf16), pltpu.VMEM((hq, feat), jnp.float32 if sum_dp else bf16)),
        in_specs=[pl.BlockSpec(memory_space=pl.ANY)] * 3,
        out_specs=[pl.BlockSpec(memory_space=pltpu.VMEM)] * 2,
        scratch_shapes=[
            pltpu.VMEM((n, chunks, tok, wide), bf16),
            pltpu.VMEM((n * tok, feat), bf16),
            pltpu.VMEM((hq, feat), bf16),
            pltpu.VMEM((n, chunks, tok, wide), bf16),
            pltpu.VMEM((2, n, chunks, tok, wide), bf16),
            pltpu.VMEM((wide, feat), jnp.float32),
            pltpu.VMEM((chunks, slots, piece, feat), bf16),
            pltpu.VMEM((chunks, slots, piece, feat), bf16),
            pltpu.VMEM((chunks, slots, piece, feat), bf16),
            dma((2 + chunks,)),
            dma((2, n, chunks)), dma((2, n, chunks)),
            dma((n_row,)), dma((n_row,)),
            dma((slots, chunks)), dma((slots, chunks)), dma((slots, chunks)), dma((slots, chunks)),
        ],
        compiler_params=pltpu.CompilerParams(
            collective_id=0, has_side_effects=True, vmem_limit_bytes=54 * 1024 * 1024),
        cost_estimate=pl.CostEstimate(
            flops=4 * n * tok * hq * feat, bytes_accessed=4 * n * tok * (hq + feat), transcendentals=0),
    )(attn_heads, out_weight, cotangent)
    if not sum_dp:
        weight_sum = lax.psum(weight_sum, "dp").astype(jnp.float32) * grad_scale
    return head_grad, weight_sum


def solution(mesh):
    return jax.shard_map(
        functools.partial(per_device, dict(mesh.shape)),
        mesh=mesh,
        in_specs=(P(("dp", "col"), "row"), P("row", "col"), P(("dp", "row"), "col")),
        out_specs=(P(("dp", "col"), "row"), P("row", "col")),
        check_vma=False,
    )
```

```python
import functools

import jax
import jax.numpy as jnp
from jax import lax
from jax.experimental import pallas as pl
from jax.experimental.pallas import tpu as pltpu
from jax.sharding import PartitionSpec as P

MESH = pl.DeviceIdType.MESH
TILE = 256


def kernel(n, n_row, n_dp, sum_dp, chunks, grad_scale, heads_ref, weight_ref, cot_ref, head_ref, wg_ref,
           heads_all, cot_all, weight, part, run, acc, wg_send, dp_recv, wg_sum, local_sem,
           z_send, z_recv, row_send, row_recv, rs_send, rs_recv, ag_send, ag_recv):
    c, r, d = lax.axis_index("col"), lax.axis_index("row"), lax.axis_index("dp")
    tok, hq = heads_ref.shape
    wide = hq // chunks
    cot_rows, feat = cot_ref.shape
    piece = wide // n_dp

    barrier = pltpu.get_barrier_semaphore()

    @pl.when(c > 0)
    def _():
        pl.semaphore_signal(barrier, inc=1, device_id={"col": c - 1}, device_id_type=MESH)

    @pl.when(c < n - 1)
    def _():
        pl.semaphore_signal(barrier, inc=1, device_id={"col": c + 1}, device_id_type=MESH)

    for o in range(1, n_row):
        pl.semaphore_signal(barrier, inc=1, device_id={"row": lax.rem(r + o, n_row)}, device_id_type=MESH)
    if sum_dp:
        for o in range(1, n_dp):
            pl.semaphore_signal(barrier, inc=1, device_id={"dp": lax.rem(d + o, n_dp)}, device_id_type=MESH)
    others = (n_row - 1) + (n_dp - 1 if sum_dp else 0)
    pl.semaphore_wait(barrier, others + (c > 0).astype(jnp.int32) + (c < n - 1).astype(jnp.int32))

    def z_copy(way, j, k, src, dst):
        to = jnp.clip(c + 1 - 2 * way, 0, n - 1)
        return pltpu.make_async_remote_copy(
            src_ref=src, dst_ref=dst, send_sem=z_send.at[way, j, k], recv_sem=z_recv.at[way, j, k],
            device_id={"col": to}, device_id_type=MESH)

    def row_copy(o):
        at = pl.ds(pl.multiple_of(r * cot_rows, cot_rows), cot_rows)
        return pltpu.make_async_remote_copy(
            src_ref=cot_ref, dst_ref=cot_all.at[at], send_sem=row_send.at[o], recv_sem=row_recv.at[o],
            device_id={"row": lax.rem(r + o, n_row)}, device_id_type=MESH)

    def heads_chunk(k):
        return heads_ref.at[:, pl.ds(k * wide, wide)]

    for k in range(chunks):
        @pl.when(c < n - 1)
        def _():
            z_copy(0, 0, k, heads_chunk(k), heads_all.at[c, k]).start()

        @pl.when(c > 0)
        def _():
            z_copy(1, 0, k, heads_chunk(k), heads_all.at[c, k]).start()

    for o in range(1, n_row):
        row_copy(o).start()
    own_cot = pltpu.make_async_copy(
        cot_ref, cot_all.at[pl.ds(pl.multiple_of(r * cot_rows, cot_rows), cot_rows)], local_sem.at[0])
    own_cot.start()
    own_weight = pltpu.make_async_copy(weight_ref, weight, local_sem.at[1])
    own_weight.start()

    own_heads = [pltpu.make_async_copy(heads_chunk(k), heads_all.at[c, k], local_sem.at[2 + k])
                 for k in range(chunks)]
    for copy in own_heads:
        copy.start()
    own_weight.wait()
    own_cot.wait()
    for o in range(1, n_row):
        row_copy(o).wait_recv()

    def partials(i, carry):
        t, m = i // (tok // TILE), lax.rem(i, tok // TILE)
        rows = pl.ds(pl.multiple_of(i * TILE, TILE), TILE)
        for k in range(chunks):
            part[t, k, pl.ds(pl.multiple_of(m * TILE, TILE), TILE), :] = lax.dot_general(
                cot_all[rows, :], weight[k * wide:(k + 1) * wide, :], (((1,), (1,)), ((), ())),
                preferred_element_type=jnp.float32).astype(jnp.bfloat16)
        return carry

    lax.fori_loop(0, n * tok // TILE, partials, 0)
    for copy in own_heads:
        copy.wait()

    def add_rows(way, j, k, t):
        def body(m, carry):
            rows = pl.ds(pl.multiple_of(m * TILE, TILE), TILE)
            run[way, j, k, rows, :] = (run[way, j, k, rows, :].astype(jnp.float32)
                                       + part[t, k, rows, :].astype(jnp.float32)).astype(jnp.bfloat16)
            return carry
        lax.fori_loop(0, tok // TILE, body, 0)

    def arrive(way, j, k):
        p = c if way == 0 else n - 1 - c

        def shard(q):
            return q if way == 0 else n - 1 - q

        @pl.when(jnp.logical_and(p > 0, j < p))
        def _():
            s = jnp.clip(shard(p - 1 - j), 0, n - 1)
            z_copy(way, j, k, heads_all.at[s, k], heads_all.at[s, k]).wait_recv()
            if j < n - 1:
                @pl.when(p < n - 1)
                def _():
                    z_copy(way, j + 1, k, heads_all.at[s, k], heads_all.at[s, k]).start()

        @pl.when(jnp.logical_and(p > 0, j >= p))
        def _():
            z_copy(way, j, k, run.at[way, j, k], run.at[way, j, k]).wait_recv()
            if j < n - 1:
                t = jnp.clip(shard(n + p - 1 - j), 0, n - 1)
                add_rows(way, j, k, t)
                z_copy(way, j + 1, k, run.at[way, j, k], run.at[way, j + 1, k]).start()

        if j < n - 1:
            @pl.when(p == 0)
            def _():
                t = shard(n - 1 - j)
                z_copy(way, j + 1, k, part.at[t, k], run.at[way, j + 1, k]).start()

    def weight_chunk(k):
        for s in range(n):
            term = lax.dot_general(
                heads_all[s, k], cot_all[s * tok:(s + 1) * tok, :], (((0,), (0,)), ((), ())),
                preferred_element_type=jnp.float32)
            if s == 0:
                acc[...] = term
            else:
                acc[...] += term
        if not sum_dp:
            wg_ref[pl.ds(pl.multiple_of(k * wide, wide), wide), :] = acc[...].astype(jnp.bfloat16)
            return
        for q in range(n_dp):
            wg_send[k, q] = acc[q * piece:(q + 1) * piece, :].astype(jnp.bfloat16)
        for o in range(1, n_dp):
            to_owner(o, k).start()

    def to_owner(o, k):
        to = lax.rem(d + o, n_dp)
        return pltpu.make_async_remote_copy(
            src_ref=wg_send.at[k, to], dst_ref=dp_recv.at[k, o], send_sem=rs_send.at[o, k],
            recv_sem=rs_recv.at[o, k], device_id={"dp": to}, device_id_type=MESH)

    def from_owner(o, k):
        return pltpu.make_async_remote_copy(
            src_ref=wg_sum.at[k, d], dst_ref=wg_sum.at[k, d], send_sem=ag_send.at[o, k],
            recv_sem=ag_recv.at[o, k], device_id={"dp": lax.rem(d + o, n_dp)}, device_id_type=MESH)

    def own_piece(k):
        for o in range(1, n_dp):
            to_owner(o, k).wait_recv()
        total = wg_send[k, d].astype(jnp.float32)
        for o in range(1, n_dp):
            total = total + dp_recv[k, o].astype(jnp.float32)
        wg_sum[k, d] = total.astype(jnp.bfloat16)
        for o in range(1, n_dp):
            from_owner(o, k).start()

    def widen(k):
        for o in range(1, n_dp):
            from_owner(o, k).wait_recv()
        for q in range(n_dp):
            at = k * wide + q * piece
            wg_ref[at:at + piece, :] = wg_sum[k, q].astype(jnp.float32) * grad_scale

    def finish(k):
        def body(m, carry):
            rows = pl.ds(pl.multiple_of(m * TILE, TILE), TILE)
            up = jnp.where(c > 0, run[0, n - 1, k, rows, :].astype(jnp.float32), 0.0)
            down = jnp.where(c < n - 1, run[1, n - 1, k, rows, :].astype(jnp.float32), 0.0)
            total = part[c, k, rows, :].astype(jnp.float32) + up + down
            head_ref[rows, pl.ds(k * wide, wide)] = total.astype(jnp.bfloat16)
            return carry
        lax.fori_loop(0, tok // TILE, body, 0)

    def clear(way):
        for k in range(chunks):
            run[way, n - 1, k] = jnp.zeros_like(run[way, n - 1, k])

    pl.when(c == 0)(lambda: clear(0))
    pl.when(c == n - 1)(lambda: clear(1))

    for j in range(n - 1):
        def step(k, carry, j=j):
            arrive(0, j, k)
            arrive(1, j, k)
            if j == n - 2:
                weight_chunk(k)
            return carry
        lax.fori_loop(0, chunks, step, 0)

    def sent(j, k):
        @pl.when(c < n - 1)
        def _():
            z_copy(0, j, k, run.at[0, j, k], run.at[0, j, k]).wait_send()

        @pl.when(c > 0)
        def _():
            z_copy(1, j, k, run.at[1, j, k], run.at[1, j, k]).wait_send()

    def drain(k, carry):
        for j in range(n - 1):
            sent(j, k)
        if sum_dp:
            for o in range(1, n_dp):
                to_owner(o, k).wait_send()
                from_owner(o, k).wait_send()
        return carry

    for k in range(chunks):
        if sum_dp:
            for late in range(chunks):
                if max(late - 1, 0) == k:
                    own_piece(late)
            if k == chunks - 1:
                for late in range(chunks):
                    widen(late)
        if k == chunks - 1:
            lax.fori_loop(0, chunks, drain, 0)
            for o in range(1, n_row):
                row_copy(o).wait_send()
        arrive(0, n - 1, k)
        arrive(1, n - 1, k)
        finish(k)
    for k in range(chunks):
        sent(n - 1, k)


def store(head_ref, wg_ref, head_out, wg_out, sem):
    copies = [pltpu.make_async_copy(head_ref, head_out, sem.at[0])]
    half = wg_ref.shape[0] // 2
    for i in range(2):
        rows = pl.ds(i * half, half)
        copies.append(pltpu.make_async_copy(wg_ref.at[rows], wg_out.at[rows], sem.at[1 + i]))
    for copy in copies:
        copy.start()
    for copy in copies:
        copy.wait()


def per_device(sizes, attn_heads, out_weight, cotangent):
    n, n_row, n_dp = sizes["col"], sizes["row"], sizes["dp"]
    tok, hq = attn_heads.shape
    feat = out_weight.shape[1]
    chunks = 3
    wide = hq // chunks
    sum_dp = wide % (16 * n_dp) == 0
    grad_scale = float(tok * n * n_dp) ** (-0.5)
    bf16, dma = jnp.bfloat16, pltpu.SemaphoreType.DMA
    piece = wide // n_dp if sum_dp else 16
    slots = n_dp if sum_dp else 1
    head_grad, weight_sum = pl.pallas_call(
        functools.partial(kernel, n, n_row, n_dp, sum_dp, chunks, grad_scale),
        out_shape=(pltpu.VMEM((tok, hq), bf16), pltpu.VMEM((hq, feat), jnp.float32 if sum_dp else bf16)),
        in_specs=[pl.BlockSpec(memory_space=pl.ANY)] * 3,
        out_specs=[pl.BlockSpec(memory_space=pltpu.VMEM)] * 2,
        scratch_shapes=[
            pltpu.VMEM((n, chunks, tok, wide), bf16),
            pltpu.VMEM((n * tok, feat), bf16),
            pltpu.VMEM((hq, feat), bf16),
            pltpu.VMEM((n, chunks, tok, wide), bf16),
            pltpu.VMEM((2, n, chunks, tok, wide), bf16),
            pltpu.VMEM((wide, feat), jnp.float32),
            pltpu.VMEM((chunks, slots, piece, feat), bf16),
            pltpu.VMEM((chunks, slots, piece, feat), bf16),
            pltpu.VMEM((chunks, slots, piece, feat), bf16),
            dma((2 + chunks,)),
            dma((2, n, chunks)), dma((2, n, chunks)),
            dma((n_row,)), dma((n_row,)),
            dma((slots, chunks)), dma((slots, chunks)), dma((slots, chunks)), dma((slots, chunks)),
        ],
        compiler_params=pltpu.CompilerParams(
            collective_id=0, has_side_effects=True, vmem_limit_bytes=54 * 1024 * 1024),
        cost_estimate=pl.CostEstimate(
            flops=4 * n * tok * hq * feat, bytes_accessed=4 * n * tok * (hq + feat), transcendentals=0),
    )(attn_heads, out_weight, cotangent)
    if not sum_dp:
        weight_sum = lax.psum(weight_sum, "dp").astype(jnp.float32) * grad_scale
        return head_grad, weight_sum
    return pl.pallas_call(
        store,
        out_shape=(jax.ShapeDtypeStruct((tok, hq), bf16), jax.ShapeDtypeStruct((hq, feat), jnp.float32)),
        in_specs=[pl.BlockSpec(memory_space=pltpu.VMEM)] * 2,
        out_specs=[pl.BlockSpec(memory_space=pl.ANY)] * 2,
        scratch_shapes=[dma((3,))],
        compiler_params=pltpu.CompilerParams(vmem_limit_bytes=16 * 1024 * 1024),
    )(head_grad, weight_sum)


def solution(mesh):
    return jax.shard_map(
        functools.partial(per_device, dict(mesh.shape)),
        mesh=mesh,
        in_specs=(P(("dp", "col"), "row"), P("row", "col"), P(("dp", "row"), "col")),
        out_specs=(P(("dp", "col"), "row"), P("row", "col")),
        check_vma=False,
    )
```

```python
import functools

import jax
import jax.numpy as jnp
from jax import lax
from jax.experimental import pallas as pl
from jax.experimental.pallas import tpu as pltpu
from jax.sharding import PartitionSpec as P

MESH = pl.DeviceIdType.MESH
TILE = 256


def kernel(n, n_row, n_dp, sum_dp, chunks, grad_scale, heads_ref, weight_ref, cot_ref, head_ref, wg_ref,
           heads_all, cot_all, weight, part, run, acc, wg_send, dp_recv, wg_sum, local_sem,
           z_send, z_recv, row_send, row_recv, rs_send, rs_recv, ag_send, ag_recv):
    c, r, d = lax.axis_index("col"), lax.axis_index("row"), lax.axis_index("dp")
    tok, hq = heads_ref.shape
    wide = hq // chunks
    cot_rows, feat = cot_ref.shape
    piece = wide // n_dp

    barrier = pltpu.get_barrier_semaphore()

    @pl.when(c > 0)
    def _():
        pl.semaphore_signal(barrier, inc=1, device_id={"col": c - 1}, device_id_type=MESH)

    @pl.when(c < n - 1)
    def _():
        pl.semaphore_signal(barrier, inc=1, device_id={"col": c + 1}, device_id_type=MESH)

    for o in range(1, n_row):
        pl.semaphore_signal(barrier, inc=1, device_id={"row": lax.rem(r + o, n_row)}, device_id_type=MESH)
    if sum_dp:
        for o in range(1, n_dp):
            pl.semaphore_signal(barrier, inc=1, device_id={"dp": lax.rem(d + o, n_dp)}, device_id_type=MESH)
    others = (n_row - 1) + (n_dp - 1 if sum_dp else 0)
    pl.semaphore_wait(barrier, others + (c > 0).astype(jnp.int32) + (c < n - 1).astype(jnp.int32))

    def z_copy(way, j, k, src, dst):
        to = jnp.clip(c + 1 - 2 * way, 0, n - 1)
        return pltpu.make_async_remote_copy(
            src_ref=src, dst_ref=dst, send_sem=z_send.at[way, j, k], recv_sem=z_recv.at[way, j, k],
            device_id={"col": to}, device_id_type=MESH)

    def row_copy(o):
        at = pl.ds(pl.multiple_of(r * cot_rows, cot_rows), cot_rows)
        return pltpu.make_async_remote_copy(
            src_ref=cot_ref, dst_ref=cot_all.at[at], send_sem=row_send.at[o], recv_sem=row_recv.at[o],
            device_id={"row": lax.rem(r + o, n_row)}, device_id_type=MESH)

    def heads_chunk(k):
        return heads_ref.at[:, pl.ds(k * wide, wide)]

    for k in range(chunks):
        @pl.when(c < n - 1)
        def _():
            z_copy(0, 0, k, heads_chunk(k), heads_all.at[c, k]).start()

        @pl.when(c > 0)
        def _():
            z_copy(1, 0, k, heads_chunk(k), heads_all.at[c, k]).start()

    for o in range(1, n_row):
        row_copy(o).start()
    own_cot = pltpu.make_async_copy(
        cot_ref, cot_all.at[pl.ds(pl.multiple_of(r * cot_rows, cot_rows), cot_rows)], local_sem.at[0])
    own_cot.start()
    own_weight = pltpu.make_async_copy(weight_ref, weight, local_sem.at[1])
    own_weight.start()

    own_heads = [pltpu.make_async_copy(heads_chunk(k), heads_all.at[c, k], local_sem.at[2 + k])
                 for k in range(chunks)]
    for copy in own_heads:
        copy.start()
    own_weight.wait()
    own_cot.wait()
    for o in range(1, n_row):
        row_copy(o).wait_recv()

    def partials(i, carry):
        t, m = i // (tok // TILE), lax.rem(i, tok // TILE)
        rows = pl.ds(pl.multiple_of(i * TILE, TILE), TILE)
        for k in range(chunks):
            part[t, k, pl.ds(pl.multiple_of(m * TILE, TILE), TILE), :] = lax.dot_general(
                cot_all[rows, :], weight[k * wide:(k + 1) * wide, :], (((1,), (1,)), ((), ())),
                preferred_element_type=jnp.float32).astype(jnp.bfloat16)
        return carry

    lax.fori_loop(0, n * tok // TILE, partials, 0)
    for copy in own_heads:
        copy.wait()

    def add_rows(way, j, k, t):
        def body(m, carry):
            rows = pl.ds(pl.multiple_of(m * TILE, TILE), TILE)
            run[way, j, k, rows, :] = (run[way, j, k, rows, :].astype(jnp.float32)
                                       + part[t, k, rows, :].astype(jnp.float32)).astype(jnp.bfloat16)
            return carry
        lax.fori_loop(0, tok // TILE, body, 0)

    def arrive(way, j, k):
        p = c if way == 0 else n - 1 - c

        def shard(q):
            return q if way == 0 else n - 1 - q

        @pl.when(jnp.logical_and(p > 0, j < p))
        def _():
            s = jnp.clip(shard(p - 1 - j), 0, n - 1)
            z_copy(way, j, k, heads_all.at[s, k], heads_all.at[s, k]).wait_recv()
            if j < n - 1:
                @pl.when(p < n - 1)
                def _():
                    z_copy(way, j + 1, k, heads_all.at[s, k], heads_all.at[s, k]).start()

        @pl.when(jnp.logical_and(p > 0, j >= p))
        def _():
            z_copy(way, j, k, run.at[way, j, k], run.at[way, j, k]).wait_recv()
            if j < n - 1:
                t = jnp.clip(shard(n + p - 1 - j), 0, n - 1)
                add_rows(way, j, k, t)
                z_copy(way, j + 1, k, run.at[way, j, k], run.at[way, j + 1, k]).start()

        if j < n - 1:
            @pl.when(p == 0)
            def _():
                t = shard(n - 1 - j)
                z_copy(way, j + 1, k, part.at[t, k], run.at[way, j + 1, k]).start()

    def weight_chunk(k):
        for s in range(n):
            term = lax.dot_general(
                heads_all[s, k], cot_all[s * tok:(s + 1) * tok, :], (((0,), (0,)), ((), ())),
                preferred_element_type=jnp.float32)
            if s == 0:
                acc[...] = term
            else:
                acc[...] += term
        if not sum_dp:
            wg_ref[pl.ds(pl.multiple_of(k * wide, wide), wide), :] = acc[...].astype(jnp.bfloat16)
            return
        for q in range(n_dp):
            wg_send[k, q] = acc[q * piece:(q + 1) * piece, :].astype(jnp.bfloat16)
        for o in range(1, n_dp):
            to_owner(o, k).start()

    def to_owner(o, k):
        to = lax.rem(d + o, n_dp)
        return pltpu.make_async_remote_copy(
            src_ref=wg_send.at[k, to], dst_ref=dp_recv.at[k, o], send_sem=rs_send.at[o, k],
            recv_sem=rs_recv.at[o, k], device_id={"dp": to}, device_id_type=MESH)

    def from_owner(o, k):
        return pltpu.make_async_remote_copy(
            src_ref=wg_sum.at[k, d], dst_ref=wg_sum.at[k, d], send_sem=ag_send.at[o, k],
            recv_sem=ag_recv.at[o, k], device_id={"dp": lax.rem(d + o, n_dp)}, device_id_type=MESH)

    def own_piece(k):
        for o in range(1, n_dp):
            to_owner(o, k).wait_recv()
        total = wg_send[k, d].astype(jnp.float32)
        for o in range(1, n_dp):
            total = total + dp_recv[k, o].astype(jnp.float32)
        wg_sum[k, d] = total.astype(jnp.bfloat16)
        for o in range(1, n_dp):
            from_owner(o, k).start()

    def widen(k):
        for o in range(1, n_dp):
            from_owner(o, k).wait_recv()
        for q in range(n_dp):
            at = k * wide + q * piece
            wg_ref[at:at + piece, :] = wg_sum[k, q].astype(jnp.float32) * grad_scale

    def finish(k):
        def body(m, carry):
            rows = pl.ds(pl.multiple_of(m * TILE, TILE), TILE)
            up = jnp.where(c > 0, run[0, n - 1, k, rows, :].astype(jnp.float32), 0.0)
            down = jnp.where(c < n - 1, run[1, n - 1, k, rows, :].astype(jnp.float32), 0.0)
            total = part[c, k, rows, :].astype(jnp.float32) + up + down
            head_ref[rows, pl.ds(k * wide, wide)] = total.astype(jnp.bfloat16)
            return carry
        lax.fori_loop(0, tok // TILE, body, 0)

    def clear(way):
        for k in range(chunks):
            run[way, n - 1, k] = jnp.zeros_like(run[way, n - 1, k])

    pl.when(c == 0)(lambda: clear(0))
    pl.when(c == n - 1)(lambda: clear(1))

    for j in range(n - 1):
        def step(k, carry, j=j):
            arrive(0, j, k)
            arrive(1, j, k)
            if j == n - 2:
                weight_chunk(k)
            return carry
        lax.fori_loop(0, chunks, step, 0)

    def sent(j, k):
        @pl.when(c < n - 1)
        def _():
            z_copy(0, j, k, run.at[0, j, k], run.at[0, j, k]).wait_send()

        @pl.when(c > 0)
        def _():
            z_copy(1, j, k, run.at[1, j, k], run.at[1, j, k]).wait_send()

    def drain(k, carry):
        for j in range(n - 1):
            sent(j, k)
        if sum_dp:
            for o in range(1, n_dp):
                to_owner(o, k).wait_send()
                from_owner(o, k).wait_send()
        return carry

    for k in range(chunks):
        if sum_dp:
            for late in range(chunks):
                if max(late - 1, 0) == k:
                    own_piece(late)
            if k == chunks - 1:
                for late in range(chunks):
                    widen(late)
        if k == chunks - 1:
            lax.fori_loop(0, chunks, drain, 0)
            for o in range(1, n_row):
                row_copy(o).wait_send()
        arrive(0, n - 1, k)
        arrive(1, n - 1, k)
        finish(k)
    for k in range(chunks):
        sent(n - 1, k)


def store(head_ref, wg_ref, head_out, wg_out, sem):
    copies = [pltpu.make_async_copy(head_ref, head_out, sem.at[0])]
    half = wg_ref.shape[0] // 2
    for i in range(2):
        rows = pl.ds(i * half, half)
        copies.append(pltpu.make_async_copy(wg_ref.at[rows], wg_out.at[rows], sem.at[1 + i]))
    for copy in copies:
        copy.start()
    for copy in copies:
        copy.wait()


def per_device(sizes, attn_heads, out_weight, cotangent):
    n, n_row, n_dp = sizes["col"], sizes["row"], sizes["dp"]
    tok, hq = attn_heads.shape
    feat = out_weight.shape[1]
    chunks = hq // 128
    wide = hq // chunks
    sum_dp = wide % (16 * n_dp) == 0
    grad_scale = float(tok * n * n_dp) ** (-0.5)
    bf16, dma = jnp.bfloat16, pltpu.SemaphoreType.DMA
    piece = wide // n_dp if sum_dp else 16
    slots = n_dp if sum_dp else 1
    head_grad, weight_sum = pl.pallas_call(
        functools.partial(kernel, n, n_row, n_dp, sum_dp, chunks, grad_scale),
        out_shape=(pltpu.VMEM((tok, hq), bf16), pltpu.VMEM((hq, feat), jnp.float32 if sum_dp else bf16)),
        in_specs=[pl.BlockSpec(memory_space=pl.ANY)] * 3,
        out_specs=[pl.BlockSpec(memory_space=pltpu.VMEM)] * 2,
        scratch_shapes=[
            pltpu.VMEM((n, chunks, tok, wide), bf16),
            pltpu.VMEM((n * tok, feat), bf16),
            pltpu.VMEM((hq, feat), bf16),
            pltpu.VMEM((n, chunks, tok, wide), bf16),
            pltpu.VMEM((2, n, chunks, tok, wide), bf16),
            pltpu.VMEM((wide, feat), jnp.float32),
            pltpu.VMEM((chunks, slots, piece, feat), bf16),
            pltpu.VMEM((chunks, slots, piece, feat), bf16),
            pltpu.VMEM((chunks, slots, piece, feat), bf16),
            dma((2 + chunks,)),
            dma((2, n, chunks)), dma((2, n, chunks)),
            dma((n_row,)), dma((n_row,)),
            dma((slots, chunks)), dma((slots, chunks)), dma((slots, chunks)), dma((slots, chunks)),
        ],
        compiler_params=pltpu.CompilerParams(
            collective_id=0, has_side_effects=True, vmem_limit_bytes=54 * 1024 * 1024),
        cost_estimate=pl.CostEstimate(
            flops=4 * n * tok * hq * feat, bytes_accessed=4 * n * tok * (hq + feat), transcendentals=0),
    )(attn_heads, out_weight, cotangent)
    if not sum_dp:
        weight_sum = lax.psum(weight_sum, "dp").astype(jnp.float32) * grad_scale
        return head_grad, weight_sum
    return pl.pallas_call(
        store,
        out_shape=(jax.ShapeDtypeStruct((tok, hq), bf16), jax.ShapeDtypeStruct((hq, feat), jnp.float32)),
        in_specs=[pl.BlockSpec(memory_space=pltpu.VMEM)] * 2,
        out_specs=[pl.BlockSpec(memory_space=pl.ANY)] * 2,
        scratch_shapes=[dma((3,))],
        compiler_params=pltpu.CompilerParams(vmem_limit_bytes=16 * 1024 * 1024),
    )(head_grad, weight_sum)


def solution(mesh):
    return jax.shard_map(
        functools.partial(per_device, dict(mesh.shape)),
        mesh=mesh,
        in_specs=(P(("dp", "col"), "row"), P("row", "col"), P(("dp", "row"), "col")),
        out_specs=(P(("dp", "col"), "row"), P("row", "col")),
        check_vma=False,
    )
```
